32 devices in a mesh: scene: 2 (over x), aperture: 16 (over z, y, core).
Axes of the slice: x: 2, y: 2, z: 4, core: 2. Of those that a mesh axis runs over, the one named last changes fastest.
Arguments:
- subimages: bfloat16 [32, 2, 32, 16384], P(('scene', 'aperture')), parts along dimension 0, may hold values from -6 to 6
- range_shift: int32 [32], P(('scene', 'aperture')), parts along dimension 0, may hold values from 0 to 63, as said below
- interp_weights: bfloat16 [3, 32, 2, 64, 8], P(None, 'scene'), parts along dimension 1, may hold values from -1.5 to 1.5
- band_start: int32 [3, 32, 64], P(None, 'scene'), parts along dimension 1, may hold values from 0 to 24
- phase_params: float32 [3, 32, 2], P(None, 'scene'), parts along dimension 1, may hold values from -6 to 6
- block_owner: int32 [32], P('scene'), parts along dimension 0, may hold values from 0 to 15, each once
- group_phase: float32 [32, 2, 1024], P(('scene', 'aperture')), parts along dimension 0, may hold values from -3.140625 to 3.140625
Outputs:
- final_image: bfloat16 [32, 2, 32, 8, 1024], P(('scene', 'aperture')), parts along dimension 0
The draws below stay inside these ranges and needn't reach their ends.
There are 2 independent parts, one for each index of `scene`. The reference program is written for one: setup_inputs(seed, part) draws one part's arguments, and reference() takes and returns one part's arrays. A program takes and returns all parts, laid end to end along the dimension named above; each array names one. Nothing has to cross between parts.
Inputs may be any that keep to these rules, and one draw needn't show every extreme that they name: `range_shift`: some subimage has the offset 64 - 1. `band_start`: a band lies within the input beams. `block_owner`: each range block is held by exactly one device.
All inputs are finite; a program needn't handle non-finite values.
Results may differ from the reference program's by a relative error of at most 0.0064.
Values may be sent and summed in bfloat16 or wider, within the bound.
A program may use at most 64 MiB of HBM per device.

```python
import jax
import jax.numpy as jnp
from jax import lax

RANGE = 16384
BEAMS = 32
TAPS = 8
SECTIONS = 3
MAXOFF = 64
GROUPS = 2
BLOCK = 1024
N_APERTURE = 16


def draw_range_shift(key, part):
    key = jax.random.fold_in(key, 11)
    first_key, second_key = jax.random.split(key)
    values = jax.random.randint(first_key, (N_APERTURE,), 0, MAXOFF, dtype=jnp.int32)
    chosen = jax.random.randint(second_key, (), 0, N_APERTURE, dtype=jnp.int32)
    return values.at[chosen].set(MAXOFF - 1)


def plant(drawn, rng, low, high):
    dims = drawn.shape
    index_at = [jax.random.randint(jax.random.fold_in(rng, axis), (), 0, dims[axis]) for axis in range(len(dims))]
    drawn = drawn.at[tuple(index_at)].set(low)
    longest = dims.index(max(dims))
    index_at[longest] = (index_at[longest] + 1) % dims[longest]
    return drawn.at[tuple(index_at)].set(high)


def steps_of(rng, extent, shards, least, top_value):
    level = 1.0
    for axis_at, shards_of in shards:
        draws = jax.random.uniform(jax.random.fold_in(jax.random.fold_in(rng, 6), axis_at), (shards_of,), jnp.float32, least / len(shards), top_value / len(shards))
        level = level * jnp.repeat(jnp.exp(draws), extent[axis_at] // shards_of).reshape((-1,) + (1,) * (len(extent) - 1 - axis_at))
    return level


def centred(own_key, shape, scale, bound, shards=(), kind=jnp.bfloat16):
    loudness = steps_of(own_key, shape, shards, -0.22, 0.18) if shards else 1.0
    array = jax.random.normal(own_key, shape, jnp.float32) * scale * loudness
    return jnp.minimum(jnp.maximum(array, -bound), bound).astype(kind)


def setup_inputs(seed: int = 0, part: int = 0) -> dict:
    splits = jax.random.split(jax.random.key(seed), 8)
    part_keys = jax.random.split(jax.random.fold_in(splits[7], part), 8)
    subimages = centred(part_keys[0], (N_APERTURE, 2, BEAMS, RANGE), 1.0, 6.0, ((0, 16),))
    range_shift = draw_range_shift(jax.random.fold_in(jax.random.fold_in(splits[7], part), 71), part)
    interp_weights = centred(part_keys[2], (SECTIONS, N_APERTURE, 2, 2 * BEAMS, TAPS), (2 * TAPS) ** -0.5, 1.5)
    band_start = plant(jax.random.randint(part_keys[3], (SECTIONS, N_APERTURE, 2 * BEAMS), 0, BEAMS - TAPS + 1), jax.random.fold_in(part_keys[3], 1), 0, BEAMS - TAPS).astype(jnp.int32)
    phase_params = jnp.clip(jax.random.uniform(part_keys[4], (SECTIONS, N_APERTURE, 2), jnp.float32, -6.0, 6.0), -6.0, 6.0)
    block_owner = jax.random.permutation(part_keys[5], N_APERTURE).astype(jnp.int32)
    group_phase = jnp.clip(jax.random.uniform(part_keys[6], (N_APERTURE, GROUPS, BLOCK), jnp.float32, -3.140625, 3.140625), -3.140625, 3.140625)
    return dict(subimages=subimages, range_shift=range_shift, interp_weights=interp_weights, band_start=band_start, phase_params=phase_params, block_owner=block_owner, group_phase=group_phase)


HALF_ROOT = 0.7071067811865476


def band_matrix(tap_weights, tap_starts, columns):
    column_ids = jnp.arange(columns, dtype=jnp.int32)
    tap_ids = jnp.arange(tap_weights.shape[-1], dtype=jnp.int32)
    targets = tap_starts.astype(jnp.int32)[:, None] + tap_ids[None, :]
    hits = targets[:, :, None] == column_ids[None, None, :]
    return jnp.sum(jnp.where(hits[None], tap_weights[:, :, :, None], jnp.zeros((), tap_weights.dtype)), axis=2)


def stacked_operator(band_dense):
    upper = jnp.concatenate([band_dense[0], -band_dense[1]], axis=1)
    lower = jnp.concatenate([band_dense[1], band_dense[0]], axis=1)
    return jnp.concatenate([upper, lower], axis=0)


def phase_turn(values, params, range_count):
    positions = jnp.arange(range_count, dtype=jnp.float32) / range_count
    phase_angle = params[0] * positions + params[1]
    cosine = jnp.cos(phase_angle)
    sine_part = jnp.sin(phase_angle)
    return jnp.stack([values[0] * cosine - values[1] * sine_part, values[0] * sine_part + values[1] * cosine])


def contribution(tap_weights, tap_starts, params, image, which_half, beam_count):
    row_weights = lax.dynamic_slice_in_dim(tap_weights, (which_half * beam_count).astype(jnp.int32), beam_count, 1)
    row_starts = lax.dynamic_slice_in_dim(tap_starts, (which_half * beam_count).astype(jnp.int32), beam_count, 0)
    block_matrix = stacked_operator(band_matrix(row_weights, row_starts, beam_count))
    range_count = image.shape[2]
    product = jnp.dot(block_matrix, image.reshape(2 * beam_count, range_count), preferred_element_type=jnp.float32)
    return phase_turn(product.reshape(2, beam_count, range_count), params, range_count)


def reference(subimages, range_shift, interp_weights, band_start, phase_params, block_owner, group_phase):
    device_count = subimages.shape[0]
    beam_count = subimages.shape[2]
    range_count = subimages.shape[3]
    padded = jnp.pad(subimages, ((0, 0), (0, 0), (0, 0), (MAXOFF, 0)))
    indices = jnp.arange(device_count, dtype=jnp.int32)

    def shift_one(position):
        start = (MAXOFF - range_shift[position]).astype(jnp.int32)
        return lax.dynamic_slice_in_dim(padded[position], start, range_count, 2)

    images = lax.map(shift_one, indices)
    for level in range(SECTIONS):
        def merge_one(position, level=level, images=images):
            partner = jnp.bitwise_xor(position, 1 << level).astype(jnp.int32)
            which_half = jnp.bitwise_and(jnp.right_shift(position, level), 1).astype(jnp.int32)
            local_part = contribution(interp_weights[level, position], band_start[level, position], phase_params[level, position], images[position], which_half, beam_count)
            remote_part = contribution(interp_weights[level, partner], band_start[level, partner], phase_params[level, partner], images[partner], which_half, beam_count)
            return ((local_part + remote_part) * HALF_ROOT).astype(jnp.bfloat16)

        images = lax.map(merge_one, indices)
    sectors = 2 ** SECTIONS
    groups = device_count // sectors
    block = range_count // device_count

    def gather_block(position):
        start = (block_owner[position] * block).astype(jnp.int32)
        pieces = lax.dynamic_slice_in_dim(images, start, block, 3).astype(jnp.float32)
        pieces = pieces.reshape(groups, sectors, 2, beam_count, block)
        cosine = jnp.cos(group_phase[position])[:, None, None, :]
        sine_part = jnp.sin(group_phase[position])[:, None, None, :]
        real_part = jnp.sum(pieces[:, :, 0] * cosine - pieces[:, :, 1] * sine_part, axis=0)
        imag_part = jnp.sum(pieces[:, :, 0] * sine_part + pieces[:, :, 1] * cosine, axis=0)
        result = jnp.stack([real_part, imag_part]) * (1.0 / (groups ** 0.5))
        return jnp.transpose(result, (0, 2, 1, 3)).astype(jnp.bfloat16)

    return lax.map(gather_block, indices)
```

```python
import jax
import jax.numpy as jnp
from jax import lax
from jax.sharding import PartitionSpec as P

SECTIONS = 3
MAXOFF = 64
HALF_ROOT = 0.7071067811865476


def band_matrices(weights, starts, columns):
    column_ids = jnp.arange(columns, dtype=jnp.int32)
    tap_ids = jnp.arange(weights.shape[-1], dtype=jnp.int32)
    targets = starts[..., None] + tap_ids
    hits = targets[..., None] == column_ids
    dense = jnp.sum(
        jnp.where(hits[:, None], weights[..., None], jnp.zeros((), weights.dtype)), axis=3
    )
    upper = jnp.concatenate([dense[:, 0], -dense[:, 1]], axis=2)
    lower = jnp.concatenate([dense[:, 1], dense[:, 0]], axis=2)
    return jnp.concatenate([upper, lower], axis=1)


def shards(
    subimages, range_shift, interp_weights, band_start, phase_params, block_owner, group_phase
):
    local_image = subimages[0]
    beams = local_image.shape[1]
    range_count = local_image.shape[2]
    count = lax.axis_size("aperture")
    me = lax.axis_index("aperture")
    block = range_count // count
    groups = group_phase.shape[1]
    sectors = 2**SECTIONS
    padded = jnp.pad(local_image, ((0, 0), (0, 0), (MAXOFF, 0)))
    image = lax.dynamic_slice_in_dim(padded, MAXOFF - range_shift[0], range_count, 2)
    blocks = image.reshape(2, beams, count, block)
    outgoing = jnp.transpose(jnp.take(blocks, block_owner, axis=2), (2, 0, 1, 3))
    images = lax.all_to_all(outgoing, "aperture", split_axis=0, concat_axis=0, tiled=True)
    first = block_owner[me] * block
    positions = (first + jnp.arange(block, dtype=jnp.int32)).astype(jnp.float32) / range_count
    for level in range(SECTIONS):
        operator = band_matrices(interp_weights[level], band_start[level], beams)
        product = jnp.einsum(
            "pjk,pkr->pjr",
            operator,
            images.reshape(count, 2 * beams, block),
            preferred_element_type=jnp.float32,
        ).reshape(count, 2, 2 * beams, block)
        angle = phase_params[level][:, 0:1] * positions + phase_params[level][:, 1:2]
        cosine = jnp.cos(angle)[:, None]
        sine = jnp.sin(angle)[:, None]
        real = product[:, 0] * cosine - product[:, 1] * sine
        imag = product[:, 0] * sine + product[:, 1] * cosine
        turned = jnp.stack([real, imag], axis=1)
        step = 1 << level
        pairs = turned.reshape(count // (2 * step), 2, step, 2, 2, beams, block)
        merged = ((pairs[:, 0] + pairs[:, 1]) * HALF_ROOT).astype(jnp.bfloat16)
        images = jnp.transpose(merged, (0, 3, 1, 2, 4, 5)).reshape(count, 2, beams, block)
    pieces = images.astype(jnp.float32).reshape(groups, sectors, 2, beams, block)
    cosine = jnp.cos(group_phase[0])[:, None, None, :]
    sine = jnp.sin(group_phase[0])[:, None, None, :]
    real = jnp.sum(pieces[:, :, 0] * cosine - pieces[:, :, 1] * sine, axis=0)
    imag = jnp.sum(pieces[:, :, 0] * sine + pieces[:, :, 1] * cosine, axis=0)
    result = jnp.stack([real, imag]) * (1.0 / groups**0.5)
    return jnp.transpose(result, (0, 2, 1, 3))[None].astype(jnp.bfloat16)


def solution(mesh):
    placed = (
        P(("scene", "aperture"), None, None, None),
        P(("scene", "aperture")),
        P(None, "scene", None, None, None),
        P(None, "scene", None),
        P(None, "scene", None),
        P("scene"),
        P(("scene", "aperture"), None, None),
    )
    return jax.shard_map(
        shards,
        mesh=mesh,
        in_specs=placed,
        out_specs=P(("scene", "aperture"), None, None, None, None),
        check_vma=False,
    )
```

```python
import functools

import jax
import jax.numpy as jnp
from jax import lax
from jax.experimental import pallas as pl
from jax.experimental.pallas import tpu as pltpu
from jax.sharding import PartitionSpec as P

SECTIONS = 3
SECTORS = 2**SECTIONS
HALF_ROOT = 0.7071067811865476
LANES = 128
MESH = pl.DeviceIdType.MESH


def fill_operators(count, weights, starts_ref, operators):
    beams = operators.shape[2] // 4
    taps = weights.shape[3]
    beam = lax.broadcasted_iota(jnp.int32, (beams, 4 * beams), 0)

    for level in range(SECTIONS):
        step = 1 << level

        def pair(i, carry, level=level, step=step):
            low = (i // step) * (2 * step) + i % step
            columns = []
            for p in (low, low + step):
                starts = starts_ref[level, pl.ds(p, 1), :]
                offset = beam - jnp.concatenate([starts, starts], axis=1)
                real = weights[level, p, 0].astype(jnp.float32)
                imag = weights[level, p, 1].astype(jnp.float32)
                for both in ((real, imag), (-imag, real)):
                    taps_of = jnp.concatenate(both, axis=1)
                    dense = jnp.zeros(beam.shape, jnp.float32)
                    for t in range(taps):
                        dense = jnp.where(offset == t, taps_of[t : t + 1], dense)
                    columns.append(dense)
            stacked = jnp.concatenate(columns, axis=0)
            operators[level, i] = jnp.transpose(stacked).astype(jnp.bfloat16)
            return carry

        lax.fori_loop(0, count // 2, pair, 0)


def on_rows(row):
    size = row.shape[1]
    diagonal = lax.broadcasted_iota(jnp.int32, (size, size), 0) == lax.broadcasted_iota(
        jnp.int32, (size, size), 1
    )
    return jnp.sum(jnp.where(diagonal, row, 0.0), axis=1, keepdims=True)


def kernel(
    count,
    width,
    range_count,
    owner_ref,
    shift_ref,
    sub_ref,
    weights_ref,
    starts_ref,
    params_ref,
    group_ref,
    out_ref,
    local,
    columns,
    outgoing,
    incoming,
    weights,
    operators,
    cosines,
    sines,
    group_cosines,
    group_sines,
    total,
    staged,
    load_sem,
    weight_sem,
    out_sem,
    send_sem,
    recv_sem,
):
    me = lax.axis_index("aperture")
    half = count // 2
    side = me // half
    place = me % half
    block = range_count // count
    chunks = block // width
    groups = count // SECTORS
    rows = local.shape[0]
    beams = rows // 2

    load = pltpu.make_async_copy(sub_ref, local, load_sem)
    load.start()
    weight_load = pltpu.make_async_copy(weights_ref, weights, weight_sem)
    weight_load.start()
    barrier = pltpu.get_barrier_semaphore()

    def greet(j, carry):
        pl.semaphore_signal(
            barrier, inc=1, device_id={"aperture": (me + j) % count}, device_id_type=MESH
        )
        return carry

    lax.fori_loop(1, count, greet, 0)
    columns[0] = jnp.zeros((rows, LANES), jnp.bfloat16)
    load.wait()

    def split(k, carry):
        for v in range(8):
            at = k * 8 + v
            columns[at + 1] = local[:, pl.ds(pl.multiple_of(at * LANES, LANES), LANES)]
        return carry

    lax.fori_loop(0, range_count // LANES // 8, split, 0)
    pl.semaphore_wait(barrier, count - 1)

    reach = 2 * LANES
    source_bin = lax.broadcasted_iota(jnp.int32, (reach, LANES), 0)
    target_bin = lax.broadcasted_iota(jnp.int32, (reach, LANES), 1)
    move = (source_bin == target_bin + LANES - shift_ref[...]).astype(jnp.bfloat16)

    def shifted(to, c):
        first = owner_ref[to] * (block // LANES) + c * (width // LANES)
        tiles = [columns[first + v] for v in range(width // LANES + 1)]
        windows = [jnp.concatenate(tiles[v : v + 2], axis=1) for v in range(width // LANES)]
        moved = jnp.dot(
            jnp.concatenate(windows, axis=0), move, preferred_element_type=jnp.float32
        ).astype(jnp.bfloat16)
        return jnp.concatenate(
            [moved[v * rows : (v + 1) * rows] for v in range(width // LANES)], axis=1
        )

    def transfer(to, c):
        return pltpu.make_async_remote_copy(
            src_ref=outgoing.at[c, to],
            dst_ref=incoming.at[c, me],
            send_sem=send_sem.at[c, to],
            recv_sem=recv_sem.at[c, me],
            device_id={"aperture": to},
            device_id_type=MESH,
        )

    def send(to, c):
        outgoing[c, to] = shifted(to, c)
        transfer(to, c).start()

    def far(j):
        return (1 - side) * half + (place + j) % half

    def near(j):
        return side * half + (place + j) % half

    def send_chunk(c, carry):
        send(far(0), c)

        def both(j, carry):
            send(far(j), c)
            send(near(j), c)
            return carry

        lax.fori_loop(1, half, both, 0)
        return carry

    lax.fori_loop(0, chunks, send_chunk, 0)

    def keep_chunk(c, carry):
        incoming[c, me] = shifted(me, c)
        return carry

    lax.fori_loop(0, chunks, keep_chunk, 0)

    first = owner_ref[me] * block
    position = (first + lax.broadcasted_iota(jnp.int32, (1, block), 1)).astype(
        jnp.float32
    ) / range_count
    for level in range(SECTIONS):
        params = params_ref[level]
        angle = on_rows(params[0:1]) * position + on_rows(params[1:2])
        cosines[level] = jnp.cos(angle)
        sines[level] = jnp.sin(angle)
    scale = HALF_ROOT**SECTIONS / groups**0.5
    group_cosines[...] = jnp.cos(group_ref[...]) * scale
    group_sines[...] = jnp.sin(group_ref[...]) * scale
    weight_load.wait()
    fill_operators(count, weights, starts_ref, operators)

    def arrived(source, c):
        @pl.when(source != me)
        def _():
            pltpu.make_async_remote_copy(
                src_ref=outgoing.at[c, source],
                dst_ref=incoming.at[c, source],
                send_sem=send_sem.at[c, source],
                recv_sem=recv_sem.at[c, source],
                device_id={"aperture": source},
                device_id_type=MESH,
            ).wait_recv()

    def merge(g, c, is_first):
        def wait_one(s, carry):
            arrived(g * SECTORS + s, c)
            return carry

        lax.fori_loop(0, SECTORS, wait_one, 0)
        bins = pl.ds(pl.multiple_of(c * width, LANES), width)
        images = []
        for s in range(SECTORS):
            whole = incoming[c, g * SECTORS + s].astype(jnp.float32)
            images.append((whole[0:beams], whole[beams:rows]))

        def turned(image, cosine, sine):
            real, imag = image
            return real * cosine - imag * sine, real * sine + imag * cosine

        for level in range(SECTIONS):
            step = 1 << level
            merged = [None] * SECTORS
            for i in range(SECTORS // 2):
                low = (i // step) * (2 * step) + i % step
                high = low + step
                parts = []
                for s in (low, high):
                    row = pl.ds(g * SECTORS + s, 1)
                    parts += turned(images[s], cosines[level, row, bins], sines[level, row, bins])
                stacked = jnp.concatenate([part.astype(jnp.bfloat16) for part in parts], axis=0)
                product = jnp.dot(
                    operators[level, g * (SECTORS // 2) + i],
                    stacked,
                    preferred_element_type=jnp.float32,
                )
                merged[low] = (product[0:beams], product[rows : rows + beams])
                merged[high] = (product[beams:rows], product[rows + beams : 2 * rows])
            images = merged
        for s in range(SECTORS):
            row = pl.ds(g, 1)
            pieces = turned(images[s], group_cosines[row, bins], group_sines[row, bins])
            for part in range(2):
                at = pl.ds(part * beams * SECTORS + s, beams, stride=SECTORS)
                for v in range(width // LANES):
                    tile = pieces[part][:, v * LANES : (v + 1) * LANES]
                    tile_at = c * (width // LANES) + v
                    if is_first:
                        total[tile_at, at, :] = tile
                    else:
                        total[tile_at, at, :] += tile

    own = me // SECTORS

    def own_chunk(c, carry):
        merge(own, c, True)
        return carry

    lax.fori_loop(0, chunks, own_chunk, 0)

    def write(c):
        return pltpu.make_async_copy(
            staged.at[c],
            out_ref.at[:, pl.ds(pl.multiple_of(c * width, LANES), width)],
            out_sem.at[c],
        )

    def other_chunk(c, carry):
        def other_group(k, carry):
            merge((own + k) % groups, c, False)
            return carry

        lax.fori_loop(1, groups, other_group, 0)
        for v in range(width // LANES):
            staged[c, :, v * LANES : (v + 1) * LANES] = total[
                c * (width // LANES) + v
            ].astype(jnp.bfloat16)
        write(c).start()
        return carry

    lax.fori_loop(0, chunks, other_chunk, 0)

    def finish(c, carry):
        write(c).wait()

        def sent(j, carry):
            transfer((me + j) % count, c).wait_send()
            return carry

        lax.fori_loop(1, count, sent, 0)
        return carry

    lax.fori_loop(0, chunks, finish, 0)


def shards(
    subimages, range_shift, interp_weights, band_start, phase_params, block_owner, group_phase
):
    beams, range_count = subimages.shape[2:]
    count = lax.axis_size("aperture")
    block = range_count // count
    width = min(256, block)
    chunks = block // width
    groups = count // SECTORS
    rows = 2 * beams
    bf16, f32 = jnp.bfloat16, jnp.float32
    taps_first = jnp.swapaxes(interp_weights, 3, 4)
    anywhere = pl.BlockSpec(memory_space=pl.ANY)
    scalars = pl.BlockSpec(memory_space=pltpu.SMEM)
    vectors = pl.BlockSpec(memory_space=pltpu.VMEM)
    combined = pl.pallas_call(
        functools.partial(kernel, count, width, range_count),
        out_shape=jax.ShapeDtypeStruct((rows * SECTORS, block), bf16),
        in_specs=[scalars, vectors, anywhere, anywhere, vectors, vectors, vectors],
        out_specs=anywhere,
        scratch_shapes=[
            pltpu.VMEM((rows, range_count), bf16),
            pltpu.VMEM((range_count // LANES + 1, rows, LANES), bf16),
            pltpu.VMEM((chunks, count, rows, width), bf16),
            pltpu.VMEM((chunks, count, rows, width), bf16),
            pltpu.VMEM(taps_first.shape, bf16),
            pltpu.VMEM((SECTIONS, count // 2, 2 * rows, 2 * rows), bf16),
            pltpu.VMEM((SECTIONS, count, block), f32),
            pltpu.VMEM((SECTIONS, count, block), f32),
            pltpu.VMEM((groups, block), f32),
            pltpu.VMEM((groups, block), f32),
            pltpu.VMEM((block // LANES, rows * SECTORS, LANES), f32),
            pltpu.VMEM((chunks, rows * SECTORS, width), bf16),
            pltpu.SemaphoreType.DMA,
            pltpu.SemaphoreType.DMA,
            pltpu.SemaphoreType.DMA((chunks,)),
            pltpu.SemaphoreType.DMA((chunks, count)),
            pltpu.SemaphoreType.DMA((chunks, count)),
        ],
        compiler_params=pltpu.CompilerParams(
            collective_id=0, has_side_effects=True, vmem_limit_bytes=56 * 1024 * 1024
        ),
        cost_estimate=pl.CostEstimate(
            flops=SECTIONS * 4 * rows * rows * range_count,
            bytes_accessed=3 * rows * range_count,
            transcendentals=2 * (SECTIONS * count + groups) * block,
        ),
    )(
        block_owner,
        range_shift.reshape(1, 1),
        subimages.reshape(rows, range_count),
        taps_first,
        band_start,
        jnp.swapaxes(phase_params, 1, 2),
        group_phase[0],
    )
    return combined.reshape(1, 2, beams, SECTORS, block)


def solution(mesh):
    placed = (
        P(("scene", "aperture"), None, None, None),
        P(("scene", "aperture")),
        P(None, "scene", None, None, None),
        P(None, "scene", None),
        P(None, "scene", None),
        P("scene"),
        P(("scene", "aperture"), None, None),
    )
    return jax.shard_map(
        shards,
        mesh=mesh,
        in_specs=placed,
        out_specs=P(("scene", "aperture"), None, None, None, None),
        check_vma=False,
    )
```

```python
import functools

import jax
import jax.numpy as jnp
from jax import lax
from jax.experimental import pallas as pl
from jax.experimental.pallas import tpu as pltpu
from jax.sharding import PartitionSpec as P

SECTIONS = 3
SECTORS = 2**SECTIONS
HALF_ROOT = 0.7071067811865476
LANES = 128
MESH = pl.DeviceIdType.MESH


def fill_operators(count, weights, starts_ref, operators):
    beams = operators.shape[2] // 4
    taps = weights.shape[3]
    beam = lax.broadcasted_iota(jnp.int32, (beams, 4 * beams), 0)

    for level in range(SECTIONS):
        step = 1 << level

        def pair(i, carry, level=level, step=step):
            low = (i // step) * (2 * step) + i % step
            columns = []
            for p in (low, low + step):
                starts = starts_ref[level, pl.ds(p, 1), :]
                offset = beam - jnp.concatenate([starts, starts], axis=1)
                real = weights[level, p, 0].astype(jnp.float32)
                imag = weights[level, p, 1].astype(jnp.float32)
                for both in ((real, imag), (-imag, real)):
                    taps_of = jnp.concatenate(both, axis=1)
                    dense = jnp.zeros(beam.shape, jnp.float32)
                    for t in range(taps):
                        dense = jnp.where(offset == t, taps_of[t : t + 1], dense)
                    columns.append(dense)
            stacked = jnp.concatenate(columns, axis=0)
            operators[level, i] = jnp.transpose(stacked).astype(jnp.bfloat16)
            return carry

        lax.fori_loop(0, count // 2, pair, 0)


def on_rows(row):
    size = row.shape[1]
    diagonal = lax.broadcasted_iota(jnp.int32, (size, size), 0) == lax.broadcasted_iota(
        jnp.int32, (size, size), 1
    )
    return jnp.sum(jnp.where(diagonal, row, 0.0), axis=1, keepdims=True)


def kernel(
    count,
    width,
    range_count,
    owner_ref,
    shift_ref,
    sub_ref,
    weights_ref,
    starts_ref,
    params_ref,
    group_ref,
    out_ref,
    local,
    columns,
    outgoing,
    incoming,
    weights,
    operators,
    cosines,
    sines,
    group_cosines,
    group_sines,
    total,
    staged,
    load_sem,
    weight_sem,
    out_sem,
    send_sem,
    recv_sem,
):
    me = lax.axis_index("aperture")
    half = count // 2
    side = me // half
    place = me % half
    block = range_count // count
    chunks = block // width
    groups = count // SECTORS
    rows = local.shape[0]
    beams = rows // 2

    pieces = load_sem.shape[0]
    piece = range_count // pieces

    def load(k):
        bins = pl.ds(k * piece, piece)
        return pltpu.make_async_copy(sub_ref.at[:, bins], local.at[:, bins], load_sem.at[k])

    for k in range(pieces):
        load(k).start()
    weight_load = pltpu.make_async_copy(weights_ref, weights, weight_sem)
    weight_load.start()
    barrier = pltpu.get_barrier_semaphore()

    def greet(j, carry):
        pl.semaphore_signal(
            barrier, inc=1, device_id={"aperture": (me + j) % count}, device_id_type=MESH
        )
        return carry

    lax.fori_loop(1, count, greet, 0)
    columns[0] = jnp.zeros((rows, LANES), jnp.bfloat16)
    for k in range(pieces):
        load(k).wait()

        def split(i, carry, k=k):
            for v in range(8):
                at = k * (piece // LANES) + i * 8 + v
                columns[at + 1] = local[:, pl.ds(pl.multiple_of(at * LANES, LANES), LANES)]
            return carry

        lax.fori_loop(0, piece // LANES // 8, split, 0)
    pl.semaphore_wait(barrier, count - 1)

    reach = 2 * LANES
    source_bin = lax.broadcasted_iota(jnp.int32, (reach, LANES), 0)
    target_bin = lax.broadcasted_iota(jnp.int32, (reach, LANES), 1)
    move = (source_bin == target_bin + LANES - shift_ref[...]).astype(jnp.bfloat16)

    def shifted(to, c):
        first = owner_ref[to] * (block // LANES) + c * (width // LANES)
        tiles = [columns[first + v] for v in range(width // LANES + 1)]
        windows = [jnp.concatenate(tiles[v : v + 2], axis=1) for v in range(width // LANES)]
        moved = jnp.dot(
            jnp.concatenate(windows, axis=0), move, preferred_element_type=jnp.float32
        ).astype(jnp.bfloat16)
        return jnp.concatenate(
            [moved[v * rows : (v + 1) * rows] for v in range(width // LANES)], axis=1
        )

    def transfer(to, c):
        return pltpu.make_async_remote_copy(
            src_ref=outgoing.at[c, to],
            dst_ref=incoming.at[c, me],
            send_sem=send_sem,
            recv_sem=recv_sem.at[c, me],
            device_id={"aperture": to},
            device_id_type=MESH,
        )

    def send(to, c):
        outgoing[c, to] = shifted(to, c)
        transfer(to, c).start()

    quarter = count // 4
    corner = me % quarter

    def outer(j):
        return (1 - side) * 3 * quarter + (corner + j) % quarter

    def inner(j):
        return (2 - side) * quarter + (corner + j) % quarter

    def near(j):
        return side * half + (place + j) % half

    def send_first(c, carry):
        def three(j, carry):
            send(outer(j), c)
            send(near(2 * j + 1), c)
            send(near(2 * j + 2), c)
            return carry

        lax.fori_loop(0, quarter - 1, three, 0)
        send(outer(quarter - 1), c)
        send(near(half - 1), c)
        return carry

    lax.fori_loop(0, chunks, send_first, 0)

    def send_second(c, carry):
        def one(j, carry):
            send(inner(j), c)
            return carry

        lax.fori_loop(0, quarter, one, 0)
        return carry

    lax.fori_loop(0, chunks, send_second, 0)

    def keep_chunk(c, carry):
        incoming[c, me] = shifted(me, c)
        return carry

    lax.fori_loop(0, chunks, keep_chunk, 0)

    first = owner_ref[me] * block
    position = (first + lax.broadcasted_iota(jnp.int32, (1, block), 1)).astype(
        jnp.float32
    ) / range_count
    for level in range(SECTIONS):
        params = params_ref[level]
        angle = on_rows(params[0:1]) * position + on_rows(params[1:2])
        cosines[level] = jnp.cos(angle)
        sines[level] = jnp.sin(angle)
    scale = HALF_ROOT**SECTIONS / groups**0.5
    group_cosines[...] = jnp.cos(group_ref[...]) * scale
    group_sines[...] = jnp.sin(group_ref[...]) * scale
    weight_load.wait()
    fill_operators(count, weights, starts_ref, operators)

    def arrived(source, c):
        @pl.when(source != me)
        def _():
            pltpu.make_async_remote_copy(
                src_ref=outgoing.at[c, source],
                dst_ref=incoming.at[c, source],
                send_sem=send_sem,
                recv_sem=recv_sem.at[c, source],
                device_id={"aperture": source},
                device_id_type=MESH,
            ).wait_recv()

    def merge(g, c, is_first):
        def wait_one(s, carry):
            arrived(g * SECTORS + s, c)
            return carry

        lax.fori_loop(0, SECTORS, wait_one, 0)
        bins = pl.ds(pl.multiple_of(c * width, LANES), width)
        images = []
        for s in range(SECTORS):
            whole = incoming[c, g * SECTORS + s].astype(jnp.float32)
            images.append((whole[0:beams], whole[beams:rows]))

        def turned(image, cosine, sine):
            real, imag = image
            return real * cosine - imag * sine, real * sine + imag * cosine

        for level in range(SECTIONS):
            step = 1 << level
            merged = [None] * SECTORS
            for i in range(SECTORS // 2):
                low = (i // step) * (2 * step) + i % step
                high = low + step
                parts = []
                for s in (low, high):
                    row = pl.ds(g * SECTORS + s, 1)
                    parts += turned(images[s], cosines[level, row, bins], sines[level, row, bins])
                stacked = jnp.concatenate([part.astype(jnp.bfloat16) for part in parts], axis=0)
                product = jnp.dot(
                    operators[level, g * (SECTORS // 2) + i],
                    stacked,
                    preferred_element_type=jnp.float32,
                )
                merged[low] = (product[0:beams], product[rows : rows + beams])
                merged[high] = (product[beams:rows], product[rows + beams : 2 * rows])
            images = merged
        for s in range(SECTORS):
            row = pl.ds(g, 1)
            pieces = turned(images[s], group_cosines[row, bins], group_sines[row, bins])
            for part in range(2):
                at = pl.ds(part * beams * SECTORS + s, beams, stride=SECTORS)
                for v in range(width // LANES):
                    tile = pieces[part][:, v * LANES : (v + 1) * LANES]
                    tile_at = c * (width // LANES) + v
                    if is_first:
                        total[tile_at, at, :] = tile
                    else:
                        total[tile_at, at, :] += tile

    own = me // SECTORS

    def own_chunk(c, carry):
        merge(own, c, True)
        return carry

    lax.fori_loop(0, chunks, own_chunk, 0)

    def write(c):
        return pltpu.make_async_copy(
            staged.at[c],
            out_ref.at[:, pl.ds(pl.multiple_of(c * width, LANES), width)],
            out_sem.at[c],
        )

    def other_chunk(c, carry):
        def other_group(k, carry):
            merge((own + k) % groups, c, False)
            return carry

        lax.fori_loop(1, groups, other_group, 0)
        for v in range(width // LANES):
            staged[c, :, v * LANES : (v + 1) * LANES] = total[
                c * (width // LANES) + v
            ].astype(jnp.bfloat16)
        write(c).start()
        return carry

    lax.fori_loop(0, chunks, other_chunk, 0)

    def finish(c, carry):
        write(c).wait()
        return carry

    lax.fori_loop(0, chunks, finish, 0)
    every = outgoing.at[:, pl.ds(0, count - 1)]
    pltpu.make_async_copy(every, every, send_sem).wait()


def shards(
    subimages, range_shift, interp_weights, band_start, phase_params, block_owner, group_phase
):
    beams, range_count = subimages.shape[2:]
    count = lax.axis_size("aperture")
    block = range_count // count
    width = min(256, block)
    chunks = block // width
    groups = count // SECTORS
    rows = 2 * beams
    bf16, f32 = jnp.bfloat16, jnp.float32
    taps_first = jnp.swapaxes(interp_weights, 3, 4)
    anywhere = pl.BlockSpec(memory_space=pl.ANY)
    scalars = pl.BlockSpec(memory_space=pltpu.SMEM)
    vectors = pl.BlockSpec(memory_space=pltpu.VMEM)
    combined = pl.pallas_call(
        functools.partial(kernel, count, width, range_count),
        out_shape=jax.ShapeDtypeStruct((rows * SECTORS, block), bf16),
        in_specs=[scalars, vectors, anywhere, anywhere, vectors, vectors, vectors],
        out_specs=anywhere,
        scratch_shapes=[
            pltpu.VMEM((rows, range_count), bf16),
            pltpu.VMEM((range_count // LANES + 1, rows, LANES), bf16),
            pltpu.VMEM((chunks, count, rows, width), bf16),
            pltpu.VMEM((chunks, count, rows, width), bf16),
            pltpu.VMEM(taps_first.shape, bf16),
            pltpu.VMEM((SECTIONS, count // 2, 2 * rows, 2 * rows), bf16),
            pltpu.VMEM((SECTIONS, count, block), f32),
            pltpu.VMEM((SECTIONS, count, block), f32),
            pltpu.VMEM((groups, block), f32),
            pltpu.VMEM((groups, block), f32),
            pltpu.VMEM((block // LANES, rows * SECTORS, LANES), f32),
            pltpu.VMEM((chunks, rows * SECTORS, width), bf16),
            pltpu.SemaphoreType.DMA((4,)),
            pltpu.SemaphoreType.DMA,
            pltpu.SemaphoreType.DMA((chunks,)),
            pltpu.SemaphoreType.DMA,
            pltpu.SemaphoreType.DMA((chunks, count)),
        ],
        compiler_params=pltpu.CompilerParams(
            collective_id=0, has_side_effects=True, vmem_limit_bytes=56 * 1024 * 1024
        ),
        cost_estimate=pl.CostEstimate(
            flops=SECTIONS * 4 * rows * rows * range_count,
            bytes_accessed=3 * rows * range_count,
            transcendentals=2 * (SECTIONS * count + groups) * block,
        ),
    )(
        block_owner,
        range_shift.reshape(1, 1),
        subimages.reshape(rows, range_count),
        taps_first,
        band_start,
        jnp.swapaxes(phase_params, 1, 2),
        group_phase[0],
    )
    return combined.reshape(1, 2, beams, SECTORS, block)


def solution(mesh):
    placed = (
        P(("scene", "aperture"), None, None, None),
        P(("scene", "aperture")),
        P(None, "scene", None, None, None),
        P(None, "scene", None),
        P(None, "scene", None),
        P("scene"),
        P(("scene", "aperture"), None, None),
    )
    return jax.shard_map(
        shards,
        mesh=mesh,
        in_specs=placed,
        out_specs=P(("scene", "aperture"), None, None, None, None),
        check_vma=False,
    )
```

```python
import functools

import jax
import jax.numpy as jnp
from jax import lax
from jax.experimental import pallas as pl
from jax.experimental.pallas import tpu as pltpu
from jax.sharding import PartitionSpec as P

SECTIONS = 3
SECTORS = 2**SECTIONS
HALF_ROOT = 0.7071067811865476
LANES = 128
MESH = pl.DeviceIdType.MESH


def fill_operators(count, weights, starts_ref, operators):
    beams = operators.shape[2] // 4
    taps = weights.shape[3]
    beam = lax.broadcasted_iota(jnp.int32, (beams, 4 * beams), 0)

    for level in range(SECTIONS):
        step = 1 << level

        def pair(i, carry, level=level, step=step):
            low = (i // step) * (2 * step) + i % step
            columns = []
            for p in (low, low + step):
                starts = starts_ref[level, pl.ds(p, 1), :]
                offset = beam - jnp.concatenate([starts, starts], axis=1)
                real = weights[level, p, 0].astype(jnp.float32)
                imag = weights[level, p, 1].astype(jnp.float32)
                for both in ((real, imag), (-imag, real)):
                    taps_of = jnp.concatenate(both, axis=1)
                    dense = jnp.zeros(beam.shape, jnp.float32)
                    for t in range(taps):
                        dense = jnp.where(offset == t, taps_of[t : t + 1], dense)
                    columns.append(dense)
            stacked = jnp.concatenate(columns, axis=0)
            operators[level, i] = jnp.transpose(stacked).astype(jnp.bfloat16)
            return carry

        lax.fori_loop(0, count // 2, pair, 0)


def on_rows(row):
    size = row.shape[1]
    diagonal = lax.broadcasted_iota(jnp.int32, (size, size), 0) == lax.broadcasted_iota(
        jnp.int32, (size, size), 1
    )
    return jnp.sum(jnp.where(diagonal, row, 0.0), axis=1, keepdims=True)


def kernel(
    count,
    width,
    range_count,
    owner_ref,
    shift_ref,
    sub_ref,
    weights_ref,
    starts_ref,
    params_ref,
    group_ref,
    out_ref,
    local,
    columns,
    outgoing,
    incoming,
    weights,
    operators,
    cosines,
    sines,
    group_cosines,
    group_sines,
    total,
    staged,
    load_sem,
    weight_sem,
    out_sem,
    send_sem,
    recv_sem,
):
    me = lax.axis_index("aperture")
    half = count // 2
    side = me // half
    place = me % half
    block = range_count // count
    chunks = block // width
    groups = count // SECTORS
    rows = local.shape[0]
    beams = rows // 2

    pieces = load_sem.shape[0]
    piece = range_count // pieces

    def load(k):
        bins = pl.ds(k * piece, piece)
        return pltpu.make_async_copy(sub_ref.at[:, bins], local.at[:, bins], load_sem.at[k])

    for k in range(pieces):
        load(k).start()
    weight_load = pltpu.make_async_copy(weights_ref, weights, weight_sem)
    weight_load.start()
    barrier = pltpu.get_barrier_semaphore()

    def greet(j, carry):
        pl.semaphore_signal(
            barrier, inc=1, device_id={"aperture": (me + j) % count}, device_id_type=MESH
        )
        return carry

    lax.fori_loop(1, count, greet, 0)
    columns[0] = jnp.zeros((rows, LANES), jnp.bfloat16)
    for k in range(pieces):
        load(k).wait()

        def split(i, carry, k=k):
            for v in range(8):
                at = k * (piece // LANES) + i * 8 + v
                columns[at + 1] = local[:, pl.ds(pl.multiple_of(at * LANES, LANES), LANES)]
            return carry

        lax.fori_loop(0, piece // LANES // 8, split, 0)
    pl.semaphore_wait(barrier, count - 1)

    reach = 2 * LANES
    source_bin = lax.broadcasted_iota(jnp.int32, (reach, LANES), 0)
    target_bin = lax.broadcasted_iota(jnp.int32, (reach, LANES), 1)
    move = (source_bin == target_bin + LANES - shift_ref[...]).astype(jnp.bfloat16)

    def shifted(to, c):
        first = owner_ref[to] * (block // LANES) + c * (width // LANES)
        tiles = [columns[first + v] for v in range(width // LANES + 1)]
        windows = [jnp.concatenate(tiles[v : v + 2], axis=1) for v in range(width // LANES)]
        moved = jnp.dot(
            jnp.concatenate(windows, axis=0), move, preferred_element_type=jnp.float32
        ).astype(jnp.bfloat16)
        return jnp.concatenate(
            [moved[v * rows : (v + 1) * rows] for v in range(width // LANES)], axis=1
        )

    def transfer(to, c):
        return pltpu.make_async_remote_copy(
            src_ref=outgoing.at[c, to],
            dst_ref=incoming.at[c, me],
            send_sem=send_sem,
            recv_sem=recv_sem.at[c, me],
            device_id={"aperture": to},
            device_id_type=MESH,
        )

    def send(to, c):
        outgoing[c, to] = shifted(to, c)
        transfer(to, c).start()

    quarter = count // 4
    corner = me % quarter

    def outer(j):
        return (1 - side) * 3 * quarter + (corner + j) % quarter

    def inner(j):
        return (2 - side) * quarter + (corner + j) % quarter

    def near(j):
        return side * half + (place + j) % half

    def send_first(c, carry):
        def three(j, carry):
            send(outer(j), c)
            send(near(2 * j + 1), c)
            send(near(2 * j + 2), c)
            return carry

        lax.fori_loop(0, quarter - 1, three, 0)
        send(outer(quarter - 1), c)
        send(near(half - 1), c)
        return carry

    lax.fori_loop(0, chunks, send_first, 0)

    def send_second(c, carry):
        def one(j, carry):
            send(inner(j), c)
            return carry

        lax.fori_loop(0, quarter, one, 0)
        return carry

    lax.fori_loop(0, chunks, send_second, 0)

    def keep_chunk(c, carry):
        incoming[c, me] = shifted(me, c)
        return carry

    lax.fori_loop(0, chunks, keep_chunk, 0)

    first = owner_ref[me] * block
    position = (first + lax.broadcasted_iota(jnp.int32, (1, block), 1)).astype(
        jnp.float32
    ) / range_count
    for level in range(SECTIONS):
        params = params_ref[level]
        angle = on_rows(params[0:1]) * position + on_rows(params[1:2])
        cosines[level] = jnp.cos(angle)
        sines[level] = jnp.sin(angle)
    scale = HALF_ROOT**SECTIONS / groups**0.5
    group_cosines[...] = jnp.cos(group_ref[...]) * scale
    group_sines[...] = jnp.sin(group_ref[...]) * scale
    weight_load.wait()
    fill_operators(count, weights, starts_ref, operators)

    def arrived(source, c):
        @pl.when(source != me)
        def _():
            pltpu.make_async_remote_copy(
                src_ref=outgoing.at[c, source],
                dst_ref=incoming.at[c, source],
                send_sem=send_sem,
                recv_sem=recv_sem.at[c, source],
                device_id={"aperture": source},
                device_id_type=MESH,
            ).wait_recv()

    def merge(g, c, is_first):
        def wait_one(s, carry):
            arrived(g * SECTORS + s, c)
            return carry

        lax.fori_loop(0, SECTORS, wait_one, 0)
        bins = pl.ds(pl.multiple_of(c * width, LANES), width)
        images = []
        for s in range(SECTORS):
            whole = incoming[c, g * SECTORS + s].astype(jnp.float32)
            images.append((whole[0:beams], whole[beams:rows]))

        def turned(image, cosine, sine):
            real, imag = image
            return real * cosine - imag * sine, real * sine + imag * cosine

        for level in range(SECTIONS):
            step = 1 << level
            merged = [None] * SECTORS
            for i in range(SECTORS // 2):
                low = (i // step) * (2 * step) + i % step
                high = low + step
                parts = []
                for s in (low, high):
                    row = pl.ds(g * SECTORS + s, 1)
                    parts += turned(images[s], cosines[level, row, bins], sines[level, row, bins])
                stacked = jnp.concatenate([part.astype(jnp.bfloat16) for part in parts], axis=0)
                product = jnp.dot(
                    operators[level, g * (SECTORS // 2) + i],
                    stacked,
                    preferred_element_type=jnp.float32,
                )
                merged[low] = (product[0:beams], product[rows : rows + beams])
                merged[high] = (product[beams:rows], product[rows + beams : 2 * rows])
            images = merged
        for s in range(SECTORS):
            row = pl.ds(g, 1)
            pieces = turned(images[s], group_cosines[row, bins], group_sines[row, bins])
            for part in range(2):
                at = pl.ds(part * beams * SECTORS + s, beams, stride=SECTORS)
                for v in range(width // LANES):
                    tile = pieces[part][:, v * LANES : (v + 1) * LANES]
                    tile_at = c * (width // LANES) + v
                    if is_first:
                        total[tile_at, at, :] = tile
                    else:
                        total[tile_at, at, :] += tile

    own = me // SECTORS

    def own_chunk(c, carry):
        merge(own, c, True)
        return carry

    lax.fori_loop(0, chunks, own_chunk, 0)

    def write(c):
        return pltpu.make_async_copy(
            staged.at[c],
            out_ref.at[:, pl.ds(pl.multiple_of(c * width, LANES), width)],
            out_sem.at[c],
        )

    def other_chunk(c, carry):
        def other_group(k, carry):
            merge((own + k) % groups, c, False)
            return carry

        lax.fori_loop(1, groups, other_group, 0)
        for v in range(width // LANES):
            staged[c, :, v * LANES : (v + 1) * LANES] = total[
                c * (width // LANES) + v
            ].astype(jnp.bfloat16)
        write(c).start()
        return carry

    lax.fori_loop(0, chunks, other_chunk, 0)

    def finish(c, carry):
        write(c).wait()
        return carry

    lax.fori_loop(0, chunks, finish, 0)
    every = outgoing.at[:, pl.ds(0, count - 1)]
    pltpu.make_async_copy(every, every, send_sem).wait()


def hand_over(from_ref, out_ref, held, in_sems, out_sems):
    size = held.shape[1]
    pieces = held.shape[0]

    def bring(k):
        return pltpu.make_async_copy(from_ref.at[pl.ds(k * size, size)], held.at[k], in_sems.at[k])

    def put(k):
        return pltpu.make_async_copy(held.at[k], out_ref.at[pl.ds(k * size, size)], out_sems.at[k])

    for k in range(pieces):
        bring(k).start()
    for k in range(pieces):
        bring(k).wait()
        put(k).start()
    for k in range(pieces):
        put(k).wait()


def shards(
    subimages, range_shift, interp_weights, band_start, phase_params, block_owner, group_phase
):
    beams, range_count = subimages.shape[2:]
    count = lax.axis_size("aperture")
    block = range_count // count
    width = min(256, block)
    chunks = block // width
    groups = count // SECTORS
    rows = 2 * beams
    bf16, f32 = jnp.bfloat16, jnp.float32
    taps_first = jnp.swapaxes(interp_weights, 3, 4)
    anywhere = pl.BlockSpec(memory_space=pl.ANY)
    scalars = pl.BlockSpec(memory_space=pltpu.SMEM)
    vectors = pl.BlockSpec(memory_space=pltpu.VMEM)
    combined = pl.pallas_call(
        functools.partial(kernel, count, width, range_count),
        out_shape=jax.ShapeDtypeStruct((rows * SECTORS, block), bf16),
        in_specs=[scalars, vectors, anywhere, anywhere, vectors, vectors, vectors],
        out_specs=anywhere,
        scratch_shapes=[
            pltpu.VMEM((rows, range_count), bf16),
            pltpu.VMEM((range_count // LANES + 1, rows, LANES), bf16),
            pltpu.VMEM((chunks, count, rows, width), bf16),
            pltpu.VMEM((chunks, count, rows, width), bf16),
            pltpu.VMEM(taps_first.shape, bf16),
            pltpu.VMEM((SECTIONS, count // 2, 2 * rows, 2 * rows), bf16),
            pltpu.VMEM((SECTIONS, count, block), f32),
            pltpu.VMEM((SECTIONS, count, block), f32),
            pltpu.VMEM((groups, block), f32),
            pltpu.VMEM((groups, block), f32),
            pltpu.VMEM((block // LANES, rows * SECTORS, LANES), f32),
            pltpu.VMEM((chunks, rows * SECTORS, width), bf16),
            pltpu.SemaphoreType.DMA((4,)),
            pltpu.SemaphoreType.DMA,
            pltpu.SemaphoreType.DMA((chunks,)),
            pltpu.SemaphoreType.DMA,
            pltpu.SemaphoreType.DMA((chunks, count)),
        ],
        compiler_params=pltpu.CompilerParams(
            collective_id=0, has_side_effects=True, vmem_limit_bytes=56 * 1024 * 1024
        ),
        cost_estimate=pl.CostEstimate(
            flops=SECTIONS * 4 * rows * rows * range_count,
            bytes_accessed=3 * rows * range_count,
            transcendentals=2 * (SECTIONS * count + groups) * block,
        ),
    )(
        block_owner,
        range_shift.reshape(1, 1),
        subimages.reshape(rows, range_count),
        taps_first,
        band_start,
        jnp.swapaxes(phase_params, 1, 2),
        group_phase[0],
    )
    combined = pl.pallas_call(
        hand_over,
        out_shape=jax.ShapeDtypeStruct(combined.shape, bf16),
        in_specs=[anywhere],
        out_specs=anywhere,
        scratch_shapes=[
            pltpu.VMEM((4, rows * SECTORS // 4, block), bf16),
            pltpu.SemaphoreType.DMA((4,)),
            pltpu.SemaphoreType.DMA((4,)),
        ],
        compiler_params=pltpu.CompilerParams(vmem_limit_bytes=56 * 1024 * 1024),
    )(combined)
    return combined.reshape(1, 2, beams, SECTORS, block)


def solution(mesh):
    placed = (
        P(("scene", "aperture"), None, None, None),
        P(("scene", "aperture")),
        P(None, "scene", None, None, None),
        P(None, "scene", None),
        P(None, "scene", None),
        P("scene"),
        P(("scene", "aperture"), None, None),
    )
    return jax.shard_map(
        shards,
        mesh=mesh,
        in_specs=placed,
        out_specs=P(("scene", "aperture"), None, None, None, None),
        check_vma=False,
    )
```
